256 devices in a mesh: brick: 32 (over y_lo, z, core), view: 8 (over y_hi, x).
Axes of the slice: x: 4, y: 4 (y_hi: 2, y_lo: 2; y = y_hi * 2 + y_lo), z: 8, core: 2. Of those that a mesh axis runs over, the one named last changes fastest.
Arguments:
- estimate: float32 [512, 128, 128], P('brick', 'view'), may hold values from 0.5 to 2
- views_data: float32 [8, 512, 128, 128], P('view', 'brick'), may hold values from 0.5 to 2
- psf_taps: float32 [8, 3, 17], P('view'), may hold values from 0.05 to 1
- view_offsets: int32 [8, 2], P('view'), may hold values from -4 to 4
- coverage: int32 [32, 8], P('brick'), may hold values from 0 to 1, as said below
Outputs:
- deconvolved: float32 [512, 128, 128], P('brick', 'view')
The draws below stay inside these ranges and needn't reach their ends.
Inputs may be any that keep to these rules, and one draw needn't show every extreme that they name: `coverage`: every slab is covered by at least one view.
All inputs are finite; a program needn't handle non-finite values.
Results may differ from the reference program's by a relative error of at most 0.0001.
Values sent between devices are 32-bit elements; how exact they have to be, the bound alone decides.
A program may use at most 64 MiB of HBM per device.

```python
import math
import jax
import jax.numpy as jnp
from jax import lax

SZ = 16
NY = 128
NX = 128
R = 8
ITERS = 4
KW = 17
VIEWS = 8
BRICKS = 32
NZ = 512


def draw_coverage(key, part):
    first_key = jax.random.fold_in(key, 11)
    second_key = jax.random.fold_in(key, 23)
    levels = jax.random.randint(first_key, (BRICKS, VIEWS), 0, 4)
    chosen = jax.random.randint(second_key, (BRICKS, 1), 0, VIEWS)
    onehot = jnp.arange(VIEWS, dtype=jnp.int32)[None, :] == chosen
    return jnp.where((levels > 0) | onehot, 1, 0).astype(jnp.int32)


def plant(array, key, smallest, high):
    longest = array.shape.index(max(array.shape))
    spots = []
    for shift in (0, 1):
        where = [jax.random.randint(jax.random.fold_in(key, axis), (), 0, length) for axis, length in enumerate(array.shape)]
        where[longest] = (where[longest] + shift) % array.shape[longest]
        spots.append(tuple(where))
    return array.at[spots[0]].set(smallest).at[spots[1]].set(high)


def shard_levels(stream_key, dims, split, least, largest):
    loudness = 1.0
    for axis_at, parts in split:
        draws = jax.random.uniform(jax.random.fold_in(jax.random.fold_in(stream_key, 6), axis_at), (parts,), jnp.float32, least / len(split), largest / len(split))
        loudness = loudness * jnp.repeat(jnp.exp(draws), dims[axis_at] // parts).reshape((-1,) + (1,) * (len(dims) - 1 - axis_at))
    return loudness


def setup_inputs(seed: int = 0) -> dict:
    streams_of = jax.random.split(jax.random.key(seed), 6)
    estimate = jnp.clip(0.5 + 1.5 * jax.random.uniform(streams_of[0], (NZ, NY, NX), jnp.float32) ** shard_levels(streams_of[0], (NZ, NY, NX), ((0, 32), (1, 8)), -0.2, 0.2), 0.5, 2.0)
    views_data = jnp.clip(0.5 + 1.5 * jax.random.uniform(streams_of[1], (VIEWS, NZ, NY, NX), jnp.float32) ** shard_levels(streams_of[1], (VIEWS, NZ, NY, NX), ((0, 8), (1, 32)), -0.2, 0.2), 0.5, 2.0)
    psf_taps = jnp.clip(jnp.exp(math.log(1.0) - 2.9957323 * jax.random.uniform(streams_of[2], (VIEWS, 3, KW), jnp.float32) ** shard_levels(streams_of[2], (VIEWS, 3, KW), ((0, 8),), -0.2, 0.2)), 0.05, 1.0)
    view_offsets = plant(jax.random.randint(streams_of[3], (VIEWS, 2), 0 - R // 2, R // 2 + 1), jax.random.fold_in(streams_of[3], 1), 0 - R // 2, (R // 2 + 1) - 1).astype(jnp.int32)
    coverage = draw_coverage(jax.random.fold_in(streams_of[5], 71), 0)
    return {"estimate": estimate, "views_data": views_data, "psf_taps": psf_taps, "view_offsets": view_offsets, "coverage": coverage}


high = lax.Precision.HIGHEST


def make_band(row, offset, count):
    rows_at = jnp.arange(count, dtype=jnp.int32)[:, None]
    cols_at = jnp.arange(count, dtype=jnp.int32)[None, :]
    index = cols_at - rows_at + offset + R
    taps_at = jnp.arange(row.shape[0], dtype=jnp.int32)
    onehot = index[:, :, None] == taps_at[None, None, :]
    return jnp.sum(jnp.where(onehot, row[None, None, :], 0.0), axis=-1)


def along_first(volume, taps_row, mirror):
    padded = jnp.pad(volume, ((R, R), (0, 0), (0, 0)))
    total = jnp.zeros_like(volume)
    for k in range(2 * R + 1):
        start = 2 * R - k if mirror else k
        total = total + taps_row[k] * padded[start:start + volume.shape[0]]
    return total


def reference(estimate, views_data, psf_taps, view_offsets, coverage):
    taps = psf_taps / jnp.sum(psf_taps, axis=-1, keepdims=True)
    cover_cells = jnp.repeat(coverage.astype(jnp.float32), SZ, axis=0)
    count_cells = jnp.sum(cover_cells, axis=1)[:, None, None]
    current = estimate
    for step in range(ITERS):
        def one_view(view, total):
            row = taps[view]
            band_y = make_band(row[1], view_offsets[view, 0], NY)
            band_x = make_band(row[2], view_offsets[view, 1], NX)
            blurred = along_first(current, row[0], False)
            blurred = jnp.einsum('ij,zjx->zix', band_y, blurred, precision=high)
            blurred = jnp.einsum('zyj,ij->zyi', blurred, band_x, precision=high)
            ratio = views_data[view] / blurred
            back = jnp.einsum('zyi,ij->zyj', ratio, band_x, precision=high)
            back = jnp.einsum('ij,zix->zjx', band_y, back, precision=high)
            back = along_first(back, row[0], True)
            flag = lax.dynamic_index_in_dim(cover_cells, view, 1, keepdims=False)
            return total + flag[:, None, None] * jnp.log(back)
        merged = lax.fori_loop(0, VIEWS, one_view, jnp.zeros_like(current))
        current = current * jnp.exp(merged / count_cells)
    return current
```

```python
import functools

import jax
import jax.numpy as jnp
from jax import lax
from jax.experimental import pallas as pl
from jax.experimental.pallas import tpu as pltpu
from jax.sharding import PartitionSpec as P

R = 8
KW = 2 * R + 1
ITERS = 4
XS = 4
MESH = pl.DeviceIdType.MESH
BF16 = jnp.bfloat16
F32 = jnp.float32


def split(value):
    upper = value.astype(BF16)
    return upper, (value - upper.astype(F32)).astype(BF16)


def kernel(
    bricks, views, est_ref, rec_ref, taps_ref, off_ref, cov_ref, out_ref,
    own, whole, blur, back, logs, sums, fy, fx, gy, gx,
    ag_send, ag_recv, hp_send, hn_send, hp_recv, hn_recv,
    bp_send, bn_send, bp_recv, bn_recv, rs_send, rs_recv,
):
    slab, piece, width = est_ref.shape
    rows = piece * views
    brick, view = lax.axis_index("brick"), lax.axis_index("view")
    half = views // XS

    def peer(k, sign):
        dx, dy = k % XS, k // XS
        x = lax.rem(view % XS + sign * dx + XS, XS)
        y = lax.rem(view // XS + sign * dy + half, half)
        return y * XS + x

    has_prev, has_next = brick > 0, brick < bricks - 1

    barrier = pltpu.get_barrier_semaphore()
    for k in range(1, views):
        pl.semaphore_signal(barrier, inc=1, device_id=(brick, peer(k, 1)), device_id_type=MESH)

    @pl.when(has_prev)
    def _():
        pl.semaphore_signal(barrier, inc=1, device_id=(brick - 1, view), device_id_type=MESH)

    @pl.when(has_next)
    def _():
        pl.semaphore_signal(barrier, inc=1, device_id=(brick + 1, view), device_id_type=MESH)

    def total(row):
        value = taps_ref[0, row, 0]
        for k in range(1, KW):
            value = value + taps_ref[0, row, k]
        return value

    def fill(row, offset, scale, lhs, rhs_up, ref):
        r = lax.broadcasted_iota(jnp.int32, (rows, rows), 0)
        c = lax.broadcasted_iota(jnp.int32, (rows, rows), 1)
        index = (c - r if rhs_up else r - c) + offset + R
        band = jnp.zeros((rows, rows), F32)
        for k in range(KW):
            band = jnp.where(index == k, taps_ref[0, row, k], band)
        upper, lower = split(band / jnp.full((rows, rows), scale, F32))
        if lhs:
            ref[...] = jnp.concatenate(
                [jnp.concatenate([upper, upper], 1), jnp.concatenate([lower, lower], 1)], 0)
        else:
            ref[...] = jnp.concatenate(
                [jnp.concatenate([upper, lower], 1), jnp.concatenate([upper, lower], 1)], 0)

    scale_y = total(1)
    scale_x = total(2) * total(0)
    fill(1, off_ref[0, 0], scale_y, True, True, fy)
    fill(1, off_ref[0, 0], scale_y, True, False, gy)
    fill(2, off_ref[0, 1], scale_x, False, False, fx)
    fill(2, off_ref[0, 1], scale_x, False, True, gx)

    count = cov_ref[0, 0]
    for k in range(1, views):
        count = count + cov_ref[0, k]
    count = count.astype(F32)
    flag = cov_ref[0, view].astype(F32)

    @pl.when(jnp.logical_not(has_prev))
    def _():
        whole[0:R] = jnp.zeros((R, rows, width), F32)
        back[0:R] = jnp.zeros((R, rows, width), F32)

    @pl.when(jnp.logical_not(has_next))
    def _():
        whole[R + slab:] = jnp.zeros((R, rows, width), F32)
        back[R + slab:] = jnp.zeros((R, rows, width), F32)

    def at(owner):
        return pl.ds(pl.multiple_of(owner * piece, piece), piece)

    def gather(k):
        return pltpu.make_async_remote_copy(
            own, whole.at[pl.ds(R, slab), at(view)], ag_send.at[k], ag_recv.at[k],
            device_id=(brick, peer(k, 1)), device_id_type=MESH)

    def to_prev(buf, k, owner, send, recv):
        return pltpu.make_async_remote_copy(
            buf.at[pl.ds(R, R), at(owner)], buf.at[pl.ds(R + slab, R), at(owner)],
            send.at[k], recv.at[k], device_id=(brick - 1, view), device_id_type=MESH)

    def to_next(buf, k, owner, send, recv):
        return pltpu.make_async_remote_copy(
            buf.at[pl.ds(slab, R), at(owner)], buf.at[pl.ds(0, R), at(owner)],
            send.at[k], recv.at[k], device_id=(brick + 1, view), device_id_type=MESH)

    def scatter(k):
        return pltpu.make_async_remote_copy(
            logs.at[:, at(peer(k, 1))], sums.at[k], rs_send.at[k], rs_recv.at[k],
            device_id=(brick, peer(k, 1)), device_id_type=MESH)

    def convolve(buf, owner, mirror, store):
        def tile(i, carry):
            place = pl.ds(pl.multiple_of(owner * piece + i * 8, 8), 8)
            layers = [buf[z, place, :] for z in range(slab + 2 * R)]
            for z in range(slab):
                acc = None
                for k in range(KW):
                    term = taps_ref[0, 0, k] * layers[z + 2 * R - k if mirror else z + k]
                    acc = term if acc is None else acc + term
                store(z, place, i, acc)
            return carry
        lax.fori_loop(0, piece // 8, tile, 0)

    def store_blur(z, place, i, value):
        blur[z, place, :] = value

    def store_logs(z, place, i, value):
        logs[z, place, :] = flag * jnp.log(value)

    def store_own(z, place, i, value):
        sums[0, z, pl.ds(pl.multiple_of(i * 8, 8), 8), :] = flag * jnp.log(value)

    def bands(z):
        h0, l0 = split(blur[z])
        h1, l1 = split(blur[z + 1])
        data = jnp.concatenate([jnp.concatenate([h0, h1], 1), jnp.concatenate([l0, l1], 1)], 0)
        o = jnp.dot(fy[...], data, preferred_element_type=F32)
        o = o[:rows] + o[rows:]
        h, l = split(jnp.concatenate([o[:, :width], o[:, width:]], 0))
        o = jnp.dot(jnp.concatenate([h, l], 1), fx[...], preferred_element_type=F32)
        o = o[:, :width] + o[:, width:]
        recorded = jnp.concatenate([rec_ref[0, z], rec_ref[0, z + 1]], 0)
        h, l = split(recorded / o)
        o = jnp.dot(jnp.concatenate([h, l], 1), gx[...], preferred_element_type=F32)
        h, l = split(o[:, :width] + o[:, width:])
        data = jnp.concatenate(
            [jnp.concatenate([h[:rows], h[rows:]], 1), jnp.concatenate([l[:rows], l[rows:]], 1)], 0)
        o = jnp.dot(gy[...], data, preferred_element_type=F32)
        o = o[:rows] + o[rows:]
        back[R + z] = o[:, :width]
        back[R + z + 1] = o[:, width:]

    def half_bands(start):
        def pair(i, carry):
            for j in range(2):
                bands(start + 4 * i + 2 * j)
            return carry
        lax.fori_loop(0, R // 4, pair, 0)

    own[...] = est_ref[...]
    partners = views - 1 + has_prev.astype(jnp.int32) + has_next.astype(jnp.int32)
    pl.semaphore_wait(barrier, partners)

    def each(first, last, body):
        def step(k, carry):
            body(k)
            return carry
        lax.fori_loop(first, last, step, 0)

    each(1, views, lambda k: gather(k).start())

    def iteration(t, carry):
        whole[pl.ds(R, slab), at(view)] = own[...]

        def arrive(k):
            owner = peer(k, -1)

            @pl.when(k > 0)
            def _():
                gather(k).wait_recv()

            @pl.when(has_prev)
            def _():
                to_prev(whole, k, owner, hp_send, hn_recv).start()

            @pl.when(has_next)
            def _():
                to_next(whole, k, owner, hn_send, hp_recv).start()

        each(0, views, arrive)

        def forward(k):
            owner = peer(k, -1)

            @pl.when(has_next)
            def _():
                to_prev(whole, k, owner, hp_send, hn_recv).wait_recv()

            @pl.when(has_prev)
            def _():
                to_next(whole, k, owner, hn_send, hp_recv).wait_recv()
            convolve(whole, owner, False, store_blur)

        each(0, views, forward)

        def sent(k):
            owner = peer(k, -1)

            @pl.when(has_prev)
            def _():
                to_prev(whole, k, owner, hp_send, hn_recv).wait_send()

            @pl.when(has_next)
            def _():
                to_next(whole, k, owner, hn_send, hp_recv).wait_send()

        each(0, views, sent)
        each(1, views, lambda k: gather(k).wait_send())

        half_bands(0)

        @pl.when(has_prev)
        def _():
            each(1, views, lambda k: to_prev(back, k, peer(k, 1), bp_send, bn_recv).start())
            to_prev(back, 0, view, bp_send, bn_recv).start()
        half_bands(R)

        @pl.when(has_next)
        def _():
            each(1, views, lambda k: to_next(back, k, peer(k, 1), bn_send, bp_recv).start())
            to_next(back, 0, view, bn_send, bp_recv).start()

        def backward(k):
            owner = peer(k, 1)

            @pl.when(has_next)
            def _():
                to_prev(back, k, owner, bp_send, bn_recv).wait_recv()

            @pl.when(has_prev)
            def _():
                to_next(back, k, owner, bn_send, bp_recv).wait_recv()

        def backward_peer(k):
            backward(k)
            convolve(back, peer(k, 1), True, store_logs)
            scatter(k).start()

        each(1, views, backward_peer)
        backward(0)
        convolve(back, view, True, store_own)
        each(1, views, lambda k: scatter(k).wait_recv())
        merged = sums[0]
        for k in range(1, views):
            merged = merged + sums[k]
        own[...] = own[...] * jnp.exp(merged / jnp.full(merged.shape, count, F32))

        @pl.when(t < ITERS - 1)
        def _():
            each(1, views, lambda k: gather(k).start())

        each(1, views, lambda k: scatter(k).wait_send())

        def back_sent(k):
            @pl.when(has_prev)
            def _():
                to_prev(back, k, peer(k, 1), bp_send, bn_recv).wait_send()

            @pl.when(has_next)
            def _():
                to_next(back, k, peer(k, 1), bn_send, bp_recv).wait_send()

        each(0, views, back_sent)
        return carry

    lax.fori_loop(0, ITERS, iteration, 0)
    out_ref[...] = own[...]


def shards(bricks, views, estimate, views_data, psf_taps, view_offsets, coverage):
    slab, piece, width = estimate.shape
    rows = piece * views
    dma = pltpu.SemaphoreType.DMA((views,))
    return pl.pallas_call(
        functools.partial(kernel, bricks, views),
        out_shape=jax.ShapeDtypeStruct(estimate.shape, F32),
        in_specs=[pl.BlockSpec(memory_space=pltpu.VMEM)] * 2 + [pl.BlockSpec(memory_space=pltpu.SMEM)] * 3,
        out_specs=pl.BlockSpec(memory_space=pltpu.VMEM),
        scratch_shapes=[
            pltpu.VMEM((slab, piece, width), F32),
            pltpu.VMEM((slab + 2 * R, rows, width), F32),
            pltpu.VMEM((slab, rows, width), F32),
            pltpu.VMEM((slab + 2 * R, rows, width), F32),
            pltpu.VMEM((slab, rows, width), F32),
            pltpu.VMEM((views, slab, piece, width), F32),
        ] + [pltpu.VMEM((2 * rows, 2 * rows), BF16)] * 4 + [dma] * 12,
        compiler_params=pltpu.CompilerParams(
            collective_id=0, has_side_effects=True, vmem_limit_bytes=40 << 20),
        name="deconvolve",
    )(estimate, views_data, psf_taps, view_offsets, coverage)


def solution(mesh):
    return jax.shard_map(
        functools.partial(shards, mesh.shape["brick"], mesh.shape["view"]),
        mesh=mesh,
        in_specs=(
            P("brick", "view", None),
            P("view", "brick", None, None),
            P("view", None, None),
            P("view", None),
            P("brick", None),
        ),
        out_specs=P("brick", "view", None),
        check_vma=False,
    )
```

```python
import functools

import jax
import jax.numpy as jnp
from jax import lax
from jax.experimental import pallas as pl
from jax.experimental.pallas import tpu as pltpu
from jax.sharding import PartitionSpec as P

R = 8
KW = 2 * R + 1
ITERS = 4
XS = 4
ORDER = (0, 1)
LAG = 5
GATHER_BY = True
SCATTER_BY = True
GROUP = 4
MESH = pl.DeviceIdType.MESH
BF16 = jnp.bfloat16
F32 = jnp.float32


def split(value):
    upper = value.astype(BF16)
    return upper, (value - upper.astype(F32)).astype(BF16)


def kernel(
    bricks, views, est_ref, rec_hbm, taps_ref, off_ref, cov_ref, out_ref,
    rec_ref, own, whole, blur, back, logs, sums, conv, fy, fx, gy, gx,
    ag_send, ag_recv, est_send, est_recv, back_send, back_recv, rs_send, rs_recv, rec_sem,
):
    slab, piece, width = est_ref.shape
    rows = piece * views
    brick, view = lax.axis_index("brick"), lax.axis_index("view")
    half = views // XS
    core = brick % 2
    first, second = ORDER

    def peer(k, sign):
        dx, dy = k % XS, k // XS
        x = lax.rem(view % XS + sign * dx + XS, XS)
        y = lax.rem(view // XS + sign * dy + half, half)
        return y * XS + x

    begin = (R * core, R * (1 - core))
    beside = tuple(brick + start // (R // 2) - 1 for start in begin)
    exists = (jnp.logical_and(beside[0] >= 0, beside[0] < bricks), None)

    def guarded(i, body):
        if exists[i] is None:
            body()
        else:
            pl.when(exists[i])(body)

    def each(first, last, body):
        def step(k, carry):
            body(k)
            return carry
        lax.fori_loop(first, last, step, 0)

    barrier = pltpu.get_barrier_semaphore()

    def greet(target):
        pl.semaphore_signal(barrier, inc=1, device_id=target, device_id_type=MESH)

    each(1, views, lambda k: greet((brick, peer(k, 1))))
    for i in range(2):
        guarded(i, lambda: greet((beside[i], view)))

    record = pltpu.make_async_copy(rec_hbm.at[0], rec_ref, rec_sem)
    record.start()
    own[...] = est_ref[...]
    pl.semaphore_wait(barrier, views + exists[0].astype(jnp.int32))

    def at(owner):
        return pl.ds(pl.multiple_of(owner * piece, piece), piece)

    def gather(i, k):
        return pltpu.make_async_remote_copy(
            own.at[pl.ds(begin[i], R)], whole.at[pl.ds(R + begin[i], R), at(view)],
            ag_send.at[i, k], ag_recv.at[i, k], device_id=(brick, peer(k, 1)), device_id_type=MESH)

    def halo(buf, i, k, owner, send, recv):
        return pltpu.make_async_remote_copy(
            buf.at[pl.ds(R + begin[i], R), at(owner)], buf.at[pl.ds(R + slab - 3 * begin[i], R), at(owner)],
            send.at[i, k], recv.at[i, k], device_id=(beside[i], view), device_id_type=MESH)

    def est_halo(i, k):
        return halo(whole, i, k, peer(k, -1), est_send, est_recv)

    def back_halo(i, k):
        return halo(back, i, k, peer(k, 1), back_send, back_recv)

    def relay(k):
        place = whole.at[pl.ds(R + begin[first], R), at(peer(XS, 1))]
        return pltpu.make_async_remote_copy(
            place, place, ag_send.at[first, k], ag_recv.at[first, k],
            device_id=(brick, peer(k - XS, 1)), device_id_type=MESH)

    def scatter(i, k, target):
        return pltpu.make_async_remote_copy(
            logs.at[pl.ds(begin[i], R), at(peer(k, 1))], sums.at[i, k], rs_send.at[i, k], rs_recv.at[i, k],
            device_id=(brick, peer(target, 1)), device_id_type=MESH)

    def send_own(i):
        if GATHER_BY and i == first:
            each(1, XS + 1, lambda k: gather(i, XS + 1 - k).start())
        else:
            each(1, views, lambda k: gather(i, turn(k, 2)).start())

    def turn(k, shift):
        return (k + shift) % (views - 1) + 1

    for i in ORDER:
        send_own(i)

    def total(row):
        value = taps_ref[0, row, 0]
        for k in range(1, KW):
            value = value + taps_ref[0, row, k]
        return value

    def fill(row, offset, scale, lhs, rhs_up, ref):
        r = lax.broadcasted_iota(jnp.int32, (rows, rows), 0)
        c = lax.broadcasted_iota(jnp.int32, (rows, rows), 1)
        index = (c - r if rhs_up else r - c) + offset + R
        band = jnp.zeros((rows, rows), F32)
        for k in range(KW):
            band = jnp.where(index == k, taps_ref[0, row, k], band)
        upper, lower = split(band / jnp.full((rows, rows), scale, F32))
        if lhs:
            ref[...] = jnp.concatenate(
                [jnp.concatenate([upper, upper], 1), jnp.concatenate([lower, lower], 1)], 0)
        else:
            ref[...] = jnp.concatenate(
                [jnp.concatenate([upper, lower], 1), jnp.concatenate([upper, lower], 1)], 0)

    scale_y = total(1)
    scale_x = total(2) * total(0)
    fill(1, off_ref[0, 0], scale_y, True, True, fy)
    fill(1, off_ref[0, 0], scale_y, True, False, gy)
    fill(2, off_ref[0, 1], scale_x, False, False, fx)
    fill(2, off_ref[0, 1], scale_x, False, True, gx)

    count = cov_ref[0, 0]
    for k in range(1, views):
        count = count + cov_ref[0, k]
    count = count.astype(F32)
    flag = cov_ref[0, view].astype(F32)

    @pl.when(jnp.logical_not(exists[0]))
    def _():
        edge = pl.ds(R + slab - 3 * begin[1], R)
        whole[edge] = jnp.zeros((R, rows, width), F32)
        back[edge] = jnp.zeros((R, rows, width), F32)

    def convolve(buf, owner, start, layers, mirror, store):
        def tile(i, carry):
            place = pl.ds(pl.multiple_of(owner * piece + i * 8, 8), 8)
            values = [buf[start + z, place, :] for z in range(layers + 2 * R)]
            for z in range(layers):
                acc = None
                for k in range(KW):
                    term = taps_ref[0, 0, k] * values[z + 2 * R - k if mirror else z + k]
                    acc = term if acc is None else acc + term
                store(z, place, pl.ds(pl.multiple_of(i * 8, 8), 8), acc)
            return carry
        lax.fori_loop(0, piece // 8, tile, 0)

    def store_conv(z, place, local, value):
        conv[z, local, :] = value

    def along_x(value, ref):
        h, l = split(value.reshape(slab * piece, width))
        o = jnp.dot(jnp.concatenate([h, l], 1), ref[...], preferred_element_type=F32)
        return (o[:, :width] + o[:, width:]).reshape(slab, piece, width)

    def along_y(values, ref):
        parts = [split(value) for value in values]
        data = jnp.concatenate(
            [jnp.concatenate([p[0] for p in parts], 1), jnp.concatenate([p[1] for p in parts], 1)], 0)
        o = jnp.dot(ref[...], data, preferred_element_type=F32)
        o = o[:rows] + o[rows:]
        return [o[:, j * width:(j + 1) * width] for j in range(len(values))]

    def ratios(start):
        blurred = along_y([blur[start + j] for j in range(GROUP)], fy)
        ratio = [rec_ref[start + j] / blurred[j] for j in range(GROUP)]
        for j, value in enumerate(along_y(ratio, gy)):
            blur[start + j] = value

    def iteration(t, carry):
        whole[pl.ds(R, slab), at(view)] = own[...]

        def arrive(i, k):
            if not (isinstance(k, int) and k == 0):
                gather(i, k).wait_recv()
            guarded(i, lambda: est_halo(i, k).start())

        def forward(k):
            for i in ORDER:
                guarded(i, lambda: est_halo(i, k).wait_recv())
            owner = peer(k, -1)
            convolve(whole, owner, 0, slab, False, store_conv)
            blur[:, at(owner), :] = along_x(conv[...], fx)

        arrive(first, 0)
        arrive(first, XS)
        if GATHER_BY:
            each(XS + 1, views, lambda k: relay(k).start())
            each(1, XS, lambda k: arrive(first, k))
            each(XS + 1, views, lambda k: arrive(first, k))
        else:
            each(2, views, lambda k: arrive(first, turn(k, 2)))
        arrive(second, 0)

        def arrive_second(k):
            arrive(second, turn(k, 2))

            @pl.when(k == LAG)
            def _():
                forward(0)

            @pl.when(k > LAG)
            def _():
                forward(turn(k - LAG, 2))

        each(1, views, arrive_second)
        each(views - LAG, views, lambda k: forward(turn(k, 2)))

        @pl.when(t == 0)
        def _():
            record.wait()

        for start in range(0, slab, GROUP):
            ratios(start)

        def last_band(k):
            owner = peer(k, 1)
            back[pl.ds(R, slab), at(owner), :] = along_x(blur[:, at(owner), :], gx)
            for i in range(2):
                guarded(i, lambda: back_halo(i, k).start())

        each(1, views, lambda k: last_band(turn(k, 3)))
        last_band(0)

        def sent(k):
            for i in range(2):
                guarded(i, lambda: est_halo(i, k).wait_send())

        each(0, views, sent)
        for i in range(2):
            each(1, views, lambda k: gather(i, k).wait_send())

        for i in ORDER:
            def store_logs(z, place, local, value):
                logs[begin[i] + z, place, :] = flag * jnp.log(value)

            def store_own(z, place, local, value):
                sums[i, 0, z, local, :] = flag * jnp.log(value)

            def backward(k):
                guarded(i, lambda: back_halo(i, k).wait_recv())
                convolve(back, peer(k, 1), begin[i], R, True, store_logs)

            def direct(k):
                backward(k)
                scatter(i, k, k).start()

            def across(k):
                backward(k)
                scatter(i, k, k % XS).start()

            if SCATTER_BY and i == first:
                each(1, views - 1, lambda k: across(turn(k, 3)))
                backward(XS)
            else:
                each(1, views, lambda k: direct(turn(k, 3)))
            guarded(i, lambda: back_halo(i, 0).wait_recv())
            convolve(back, view, begin[i], R, True, store_own)

        if SCATTER_BY:
            each(XS + 1, views, lambda k: scatter(first, k, k).wait_recv())
            place = (pl.ds(begin[first], R), at(peer(XS, 1)))
            passed = logs[place]
            for k in range(XS + 1, views):
                passed = passed + sums[first, k]
            logs[place] = passed
            scatter(first, XS, XS).start()

        for i in ORDER:
            last = XS + 1 if SCATTER_BY and i == first else views
            each(1, last, lambda k: scatter(i, k, k).wait_recv())
            merged = sums[i, 0]
            for k in range(1, last):
                merged = merged + sums[i, k]
            mine = pl.ds(begin[i], R)
            own[mine] = own[mine] * jnp.exp(merged / jnp.full(merged.shape, count, F32))

            @pl.when(t < ITERS - 1)
            def _():
                send_own(i)

        def finished(k):
            for i in range(2):
                guarded(i, lambda: back_halo(i, k).wait_send())

        each(0, views, finished)
        for i in range(2):
            each(1, views, lambda k: scatter(i, k, k).wait_send())
        return carry

    lax.fori_loop(0, ITERS, iteration, 0)
    out_ref[...] = own[...]


def shards(bricks, views, estimate, views_data, psf_taps, view_offsets, coverage):
    slab, piece, width = estimate.shape
    rows = piece * views
    dma = pltpu.SemaphoreType.DMA((2, views))
    return pl.pallas_call(
        functools.partial(kernel, bricks, views),
        out_shape=jax.ShapeDtypeStruct(estimate.shape, F32),
        in_specs=[pl.BlockSpec(memory_space=pltpu.VMEM), pl.BlockSpec(memory_space=pl.ANY)]
        + [pl.BlockSpec(memory_space=pltpu.SMEM)] * 3,
        out_specs=pl.BlockSpec(memory_space=pltpu.VMEM),
        scratch_shapes=[
            pltpu.VMEM((slab, rows, width), F32),
            pltpu.VMEM((slab, piece, width), F32),
            pltpu.VMEM((slab + 2 * R, rows, width), F32),
            pltpu.VMEM((slab, rows, width), F32),
            pltpu.VMEM((slab + 2 * R, rows, width), F32),
            pltpu.VMEM((slab, rows, width), F32),
            pltpu.VMEM((2, views, R, piece, width), F32),
            pltpu.VMEM((slab, piece, width), F32),
        ] + [pltpu.VMEM((2 * rows, 2 * rows), BF16)] * 4 + [dma] * 8 + [pltpu.SemaphoreType.DMA],
        compiler_params=pltpu.CompilerParams(
            collective_id=0, has_side_effects=True, vmem_limit_bytes=40 << 20),
        name="deconvolve",
    )(estimate, views_data, psf_taps, view_offsets, coverage)


def solution(mesh):
    return jax.shard_map(
        functools.partial(shards, mesh.shape["brick"], mesh.shape["view"]),
        mesh=mesh,
        in_specs=(
            P("brick", "view", None),
            P("view", "brick", None, None),
            P("view", None, None),
            P("view", None),
            P("brick", None),
        ),
        out_specs=P("brick", "view", None),
        check_vma=False,
    )
```

```python
import functools

import jax
import jax.numpy as jnp
from jax import lax
from jax.experimental import pallas as pl
from jax.experimental.pallas import tpu as pltpu
from jax.sharding import PartitionSpec as P

R = 8
KW = 2 * R + 1
ITERS = 4
XS = 4
ORDER = (0, 1)
LAG = 5
EARLY = False
GATHER_BY = True
PLAN = ("1d", "1x", "1y", "2d", "2y", "2x", "1p", "1o", "2o")
GROUP = 16
MESH = pl.DeviceIdType.MESH
BF16 = jnp.bfloat16
F32 = jnp.float32


def split(value):
    upper = value.astype(BF16)
    return upper, (value - upper.astype(F32)).astype(BF16)


def kernel(
    bricks, views, est_hbm, rec_hbm, taps_ref, off_ref, cov_ref, out_ref,
    rec_ref, own, whole, blur, back, logs, sums, conv, fy, fx, gy, gx,
    ag_send, ag_recv, est_send, est_recv, back_send, back_recv, rs_send, rs_recv, est_sem, rec_sem,
):
    slab, piece, width = est_hbm.shape
    rows = piece * views
    brick, view = lax.axis_index("brick"), lax.axis_index("view")
    half = views // XS
    core = brick % 2
    first, second = ORDER

    def peer(k, sign):
        dx, dy = k % XS, k // XS
        x = lax.rem(view % XS + sign * dx + XS, XS)
        y = lax.rem(view // XS + sign * dy + half, half)
        return y * XS + x

    begin = (R * core, R * (1 - core))
    beside = tuple(brick + start // (R // 2) - 1 for start in begin)
    exists = (jnp.logical_and(beside[0] >= 0, beside[0] < bricks), None)

    def guarded(i, body):
        if exists[i] is None:
            body()
        else:
            pl.when(exists[i])(body)

    def each(first, last, body):
        def step(k, carry):
            body(k)
            return carry
        lax.fori_loop(first, last, step, 0)

    barrier = pltpu.get_barrier_semaphore()

    def greet(target):
        pl.semaphore_signal(barrier, inc=1, device_id=target, device_id_type=MESH)

    each(1, views, lambda k: greet((brick, peer(k, 1))))
    for i in range(2):
        guarded(i, lambda: greet((beside[i], view)))

    start = pltpu.make_async_copy(est_hbm, own, est_sem)
    start.start()
    record = pltpu.make_async_copy(rec_hbm.at[0], rec_ref, rec_sem)
    record.start()
    start.wait()
    pl.semaphore_wait(barrier, views + exists[0].astype(jnp.int32))

    def at(owner):
        return pl.ds(pl.multiple_of(owner * piece, piece), piece)

    def gather(i, k):
        return pltpu.make_async_remote_copy(
            own.at[pl.ds(begin[i], R)], whole.at[pl.ds(R + begin[i], R), at(view)],
            ag_send.at[i, k], ag_recv.at[i, k], device_id=(brick, peer(k, 1)), device_id_type=MESH)

    def halo(buf, i, k, owner, send, recv):
        return pltpu.make_async_remote_copy(
            buf.at[pl.ds(R + begin[i], R), at(owner)], buf.at[pl.ds(R + slab - 3 * begin[i], R), at(owner)],
            send.at[i, k], recv.at[i, k], device_id=(beside[i], view), device_id_type=MESH)

    def est_halo(i, k):
        return halo(whole, i, k, peer(k, -1), est_send, est_recv)

    def back_halo(i, k):
        return halo(back, i, k, peer(k, 1), back_send, back_recv)

    def relay(k):
        place = whole.at[pl.ds(R + begin[first], R), at(peer(XS, 1))]
        return pltpu.make_async_remote_copy(
            place, place, ag_send.at[first, k], ag_recv.at[first, k],
            device_id=(brick, peer(k - XS, 1)), device_id_type=MESH)

    def scatter(i, k, target):
        return pltpu.make_async_remote_copy(
            logs.at[pl.ds(begin[i], R), at(peer(k, 1))], sums.at[i, k], rs_send.at[i, k], rs_recv.at[i, k],
            device_id=(brick, peer(target, 1)), device_id_type=MESH)

    def send_own(i):
        whole[pl.ds(R + begin[i], R), at(view)] = own[pl.ds(begin[i], R)]
        if GATHER_BY and i == first:
            each(1, XS + 1, lambda k: gather(i, XS + 1 - k).start())
        else:
            each(1, views, lambda k: gather(i, turn(k, 6)).start())

    def turn(k, shift):
        return (k + shift) % (views - 1) + 1

    for i in ORDER:
        send_own(i)

    def total(row):
        value = taps_ref[row, 0, 0]
        for k in range(1, KW):
            value = value + taps_ref[row, 0, k]
        return value

    def fill(row, offset, scale, lhs, rhs_up, ref):
        r = lax.broadcasted_iota(jnp.int32, (rows, rows), 0)
        c = lax.broadcasted_iota(jnp.int32, (rows, rows), 1)
        index = (c - r if rhs_up else r - c) + offset + R
        band = jnp.zeros((rows, rows), F32)
        for k in range(KW):
            band = jnp.where(index == k, taps_ref[row, 0, k], band)
        upper, lower = split(band / jnp.full((rows, rows), scale, F32))
        if lhs:
            ref[...] = jnp.concatenate(
                [jnp.concatenate([upper, upper], 1), jnp.concatenate([lower, lower], 1)], 0)
        else:
            ref[...] = jnp.concatenate(
                [jnp.concatenate([upper, lower], 1), jnp.concatenate([upper, lower], 1)], 0)

    scale_y = total(1)
    scale_x = total(2) * total(0)
    fill(1, off_ref[0, 0], scale_y, True, True, fy)
    fill(1, off_ref[0, 0], scale_y, True, False, gy)
    fill(2, off_ref[0, 1], scale_x, False, False, fx)
    fill(2, off_ref[0, 1], scale_x, False, True, gx)

    count = cov_ref[0, 0]
    for k in range(1, views):
        count = count + cov_ref[0, k]
    count = count.astype(F32)
    flag = cov_ref[0, view].astype(F32)

    @pl.when(jnp.logical_not(exists[0]))
    def _():
        edge = pl.ds(R + slab - 3 * begin[1], R)
        whole[edge] = jnp.zeros((R, rows, width), F32)
        back[edge] = jnp.zeros((R, rows, width), F32)

    def convolve(buf, owner, start, layers, mirror, store):
        def tile(i, carry):
            place = pl.ds(pl.multiple_of(owner * piece + i * 8, 8), 8)
            values = [buf[start + z, place, :] for z in range(layers + 2 * R)]
            for z in range(layers):
                acc = None
                for k in range(KW):
                    term = taps_ref[0, 0, k] * values[z + 2 * R - k if mirror else z + k]
                    acc = term if acc is None else acc + term
                store(z, place, pl.ds(pl.multiple_of(i * 8, 8), 8), acc)
            return carry
        lax.fori_loop(0, piece // 8, tile, 0)

    def store_conv(z, place, local, value):
        conv[z, local, :] = value

    def along_x(value, ref):
        h, l = split(value.reshape(slab * piece, width))
        o = jnp.dot(jnp.concatenate([h, l], 1), ref[...], preferred_element_type=F32)
        return (o[:, :width] + o[:, width:]).reshape(slab, piece, width)

    def along_y(values, ref):
        parts = [split(value) for value in values]
        data = jnp.concatenate(
            [jnp.concatenate([p[0] for p in parts], 1), jnp.concatenate([p[1] for p in parts], 1)], 0)
        o = jnp.dot(ref[...], data, preferred_element_type=F32)
        o = o[:rows] + o[rows:]
        return [o[:, j * width:(j + 1) * width] for j in range(len(values))]

    def ratios(start):
        blurred = along_y([blur[start + j] for j in range(GROUP)], fy)
        ratio = [rec_ref[start + j] / blurred[j] for j in range(GROUP)]
        for j, value in enumerate(along_y(ratio, gy)):
            blur[start + j] = value

    def arrive(i, k):
        if not (isinstance(k, int) and k == 0):
            gather(i, k).wait_recv()
        guarded(i, lambda: est_halo(i, k).start())

    def arrive_across():
        arrive(first, 0)
        arrive(first, XS)
        if GATHER_BY:
            each(XS + 1, views, lambda k: relay(k).start())

    if EARLY:
        arrive_across()

    def iteration(t, carry):
        if not EARLY:
            arrive_across()

        def forward(k):
            for i in ORDER:
                guarded(i, lambda: est_halo(i, k).wait_recv())
            owner = peer(k, -1)
            convolve(whole, owner, 0, slab, False, store_conv)
            blur[:, at(owner), :] = along_x(conv[...], fx)

        if GATHER_BY:
            each(1, XS, lambda k: arrive(first, k))
            each(XS + 1, views, lambda k: arrive(first, k))
        else:
            each(2, views, lambda k: arrive(first, turn(k, 6)))
        arrive(second, 0)

        def arrive_second(k):
            arrive(second, turn(k, 6))

            @pl.when(k == LAG)
            def _():
                forward(0)

            @pl.when(k > LAG)
            def _():
                forward(turn(k - LAG, 6))

        each(1, views, arrive_second)
        each(views - LAG, views, lambda k: forward(turn(k, 6)))

        @pl.when(t == 0)
        def _():
            record.wait()

        for start in range(0, slab, GROUP):
            ratios(start)

        def last_band(k):
            owner = peer(k, 1)
            back[pl.ds(R, slab), at(owner), :] = along_x(blur[:, at(owner), :], gx)
            for i in range(2):
                guarded(i, lambda: back_halo(i, k).start())

        for k in (5, 6, 7, 1, 2, 3, 4):
            last_band(k)
        last_band(0)

        def sent(k):
            for i in range(2):
                guarded(i, lambda: est_halo(i, k).wait_send())

        each(0, views, sent)
        for i in range(2):
            each(1, views, lambda k: gather(i, k).wait_send())

        def backward(i, k, own_piece):
            def store_logs(z, place, local, value):
                logs[begin[i] + z, place, :] = flag * jnp.log(value)

            def store_own(z, place, local, value):
                sums[i, 0, z, local, :] = flag * jnp.log(value)

            guarded(i, lambda: back_halo(i, k).wait_recv())
            convolve(back, peer(k, 1), begin[i], R, True, store_own if own_piece else store_logs)

        def direct(i, k):
            backward(i, k, False)
            scatter(i, k, k).start()

        def across(k):
            backward(first, k, False)
            scatter(first, k, k % XS).start()

        def pass_on():
            each(XS + 1, views, lambda k: scatter(first, k, k).wait_recv())
            place = (pl.ds(begin[first], R), at(peer(XS, 1)))
            passed = logs[place]
            for k in range(XS + 1, views):
                passed = passed + sums[first, k]
            logs[place] = passed
            scatter(first, XS, XS).start()

        for step in PLAN:
            step_class = first if step[0] == "1" else second
            run = across if step[0] == "1" else functools.partial(direct, second)
            if step[1] == "x":
                each(1, XS, run)
            elif step[1] == "d":
                each(XS + 1, views, run)
            elif step[1] == "y" and step[0] == "1":
                backward(first, XS, False)
            elif step[1] == "y":
                run(XS)
            elif step[1] == "o":
                backward(step_class, 0, True)
            else:
                pass_on()

        for i in ORDER:
            last = XS + 1 if i == first else views
            each(1, last, lambda k: scatter(i, k, k).wait_recv())
            merged = sums[i, 0]
            for k in range(1, last):
                merged = merged + sums[i, k]
            mine = pl.ds(begin[i], R)
            own[mine] = own[mine] * jnp.exp(merged / jnp.full(merged.shape, count, F32))

            @pl.when(t < ITERS - 1)
            def _():
                send_own(i)
                if EARLY and i == first:
                    arrive_across()

        def finished(k):
            for i in range(2):
                guarded(i, lambda: back_halo(i, k).wait_send())

        each(0, views, finished)
        for i in range(2):
            each(1, views, lambda k: scatter(i, k, k).wait_send())
        return carry

    lax.fori_loop(0, ITERS, iteration, 0)
    out_ref[...] = own[...]


def shards(bricks, views, estimate, views_data, psf_taps, view_offsets, coverage):
    slab, piece, width = estimate.shape
    rows = piece * views
    dma = pltpu.SemaphoreType.DMA((2, views))
    return pl.pallas_call(
        functools.partial(kernel, bricks, views),
        out_shape=jax.ShapeDtypeStruct(estimate.shape, F32),
        in_specs=[pl.BlockSpec(memory_space=pl.ANY)] * 2
        + [pl.BlockSpec(memory_space=pltpu.SMEM)] * 3,
        out_specs=pl.BlockSpec(memory_space=pltpu.VMEM),
        scratch_shapes=[
            pltpu.VMEM((slab, rows, width), F32),
            pltpu.VMEM((slab, piece, width), F32),
            pltpu.VMEM((slab + 2 * R, rows, width), F32),
            pltpu.VMEM((slab, rows, width), F32),
            pltpu.VMEM((slab + 2 * R, rows, width), F32),
            pltpu.VMEM((slab, rows, width), F32),
            pltpu.VMEM((2, views, R, piece, width), F32),
            pltpu.VMEM((slab, piece, width), F32),
        ] + [pltpu.VMEM((2 * rows, 2 * rows), BF16)] * 4 + [dma] * 8 + [pltpu.SemaphoreType.DMA] * 2,
        compiler_params=pltpu.CompilerParams(
            collective_id=0, has_side_effects=True, vmem_limit_bytes=60 << 20),
        name="deconvolve",
    )(estimate, views_data, jnp.transpose(psf_taps, (1, 0, 2)), view_offsets, coverage)


def solution(mesh):
    return jax.shard_map(
        functools.partial(shards, mesh.shape["brick"], mesh.shape["view"]),
        mesh=mesh,
        in_specs=(
            P("brick", "view", None),
            P("view", "brick", None, None),
            P("view", None, None),
            P("view", None),
            P("brick", None),
        ),
        out_specs=P("brick", "view", None),
        check_vma=False,
    )
```

```python
import functools

import jax
import jax.numpy as jnp
from jax import lax
from jax.experimental import pallas as pl
from jax.experimental.pallas import tpu as pltpu
from jax.sharding import PartitionSpec as P

R = 8
KW = 2 * R + 1
ITERS = 4
XS = 4
ORDER = (0, 1)
LAG = 5
EARLY = False
GATHER_BY = True
PLAN = ("1d", "1x", "1y", "2d", "2y", "2x", "1p", "1o", "2o")
GROUP = 16
MESH = pl.DeviceIdType.MESH
BF16 = jnp.bfloat16
F32 = jnp.float32


def split(value):
    upper = value.astype(BF16)
    return upper, (value - upper.astype(F32)).astype(BF16)


def kernel(
    bricks, views, est_hbm, rec_hbm, taps_ref, off_ref, cov_ref, out_ref,
    rec_ref, own, whole, blur, back, logs, sums, conv, fy, fx, gy, gx,
    ag_send, ag_recv, est_send, est_recv, back_send, back_recv, rs_send, rs_recv, est_sem, rec_sem,
):
    slab, piece, width = est_hbm.shape
    rows = piece * views
    brick, view = lax.axis_index("brick"), lax.axis_index("view")
    half = views // XS
    core = brick % 2
    first, second = ORDER

    def peer(k, sign):
        dx, dy = k % XS, k // XS
        x = lax.rem(view % XS + sign * dx + XS, XS)
        y = lax.rem(view // XS + sign * dy + half, half)
        return y * XS + x

    begin = (R * core, R * (1 - core))
    beside = tuple(brick + start // (R // 2) - 1 for start in begin)
    exists = (jnp.logical_and(beside[0] >= 0, beside[0] < bricks), None)

    def guarded(i, body):
        if exists[i] is None:
            body()
        else:
            pl.when(exists[i])(body)

    def each(first, last, body):
        def step(k, carry):
            body(k)
            return carry
        lax.fori_loop(first, last, step, 0)

    barrier = pltpu.get_barrier_semaphore()

    def greet(target):
        pl.semaphore_signal(barrier, inc=1, device_id=target, device_id_type=MESH)

    each(1, views, lambda k: greet((brick, peer(k, 1))))
    for i in range(2):
        guarded(i, lambda: greet((beside[i], view)))

    start = pltpu.make_async_copy(est_hbm, own, est_sem)
    start.start()
    record = pltpu.make_async_copy(rec_hbm.at[0], rec_ref, rec_sem)
    record.start()
    start.wait()
    pl.semaphore_wait(barrier, views + exists[0].astype(jnp.int32))

    def at(owner):
        return pl.ds(pl.multiple_of(owner * piece, piece), piece)

    def gather(i, k):
        return pltpu.make_async_remote_copy(
            own.at[pl.ds(begin[i], R)], whole.at[pl.ds(R + begin[i], R), at(view)],
            ag_send.at[i, k], ag_recv.at[i, k], device_id=(brick, peer(k, 1)), device_id_type=MESH)

    def halo(buf, i, k, owner, send, recv):
        return pltpu.make_async_remote_copy(
            buf.at[pl.ds(R + begin[i], R), at(owner)], buf.at[pl.ds(R + slab - 3 * begin[i], R), at(owner)],
            send.at[i, k], recv.at[i, k], device_id=(beside[i], view), device_id_type=MESH)

    def est_halo(i, k):
        return halo(whole, i, k, peer(k, -1), est_send, est_recv)

    def back_halo(i, k):
        return halo(back, i, k, peer(k, 1), back_send, back_recv)

    def relay(k):
        place = whole.at[pl.ds(R + begin[first], R), at(peer(XS, 1))]
        return pltpu.make_async_remote_copy(
            place, place, ag_send.at[first, k], ag_recv.at[first, k],
            device_id=(brick, peer(k - XS, 1)), device_id_type=MESH)

    def scatter(i, k, target):
        return pltpu.make_async_remote_copy(
            logs.at[pl.ds(begin[i], R), at(peer(k, 1))], sums.at[i, k], rs_send.at[i, k], rs_recv.at[i, k],
            device_id=(brick, peer(target, 1)), device_id_type=MESH)

    def send_own(i):
        whole[pl.ds(R + begin[i], R), at(view)] = own[pl.ds(begin[i], R)]
        if GATHER_BY and i == first:
            each(1, XS + 1, lambda k: gather(i, XS + 1 - k).start())
        else:
            each(1, views, lambda k: gather(i, turn(k)).start())

    def turn(k):
        return (XS * k - 1) % (views - 1) + 1

    for i in ORDER:
        send_own(i)

    def total(row):
        value = taps_ref[row, 0, 0]
        for k in range(1, KW):
            value = value + taps_ref[row, 0, k]
        return value

    def fill(row, offset, scale, lhs, rhs_up, ref):
        r = lax.broadcasted_iota(jnp.int32, (rows, rows), 0)
        c = lax.broadcasted_iota(jnp.int32, (rows, rows), 1)
        index = (c - r if rhs_up else r - c) + offset + R
        band = jnp.zeros((rows, rows), F32)
        for k in range(KW):
            band = jnp.where(index == k, taps_ref[row, 0, k], band)
        upper, lower = split(band / jnp.full((rows, rows), scale, F32))
        if lhs:
            ref[...] = jnp.concatenate(
                [jnp.concatenate([upper, upper], 1), jnp.concatenate([lower, lower], 1)], 0)
        else:
            ref[...] = jnp.concatenate(
                [jnp.concatenate([upper, lower], 1), jnp.concatenate([upper, lower], 1)], 0)

    scale_y = total(1)
    scale_x = total(2) * total(0)
    fill(1, off_ref[0, 0], scale_y, True, True, fy)
    fill(1, off_ref[0, 0], scale_y, True, False, gy)
    fill(2, off_ref[0, 1], scale_x, False, False, fx)
    fill(2, off_ref[0, 1], scale_x, False, True, gx)

    count = cov_ref[0, 0]
    for k in range(1, views):
        count = count + cov_ref[0, k]
    count = count.astype(F32)
    flag = cov_ref[0, view].astype(F32)

    @pl.when(jnp.logical_not(exists[0]))
    def _():
        edge = pl.ds(R + slab - 3 * begin[1], R)
        whole[edge] = jnp.zeros((R, rows, width), F32)
        back[edge] = jnp.zeros((R, rows, width), F32)

    def convolve(buf, owner, start, layers, mirror, store):
        def tile(i, carry):
            place = pl.ds(pl.multiple_of(owner * piece + i * 8, 8), 8)
            values = [buf[start + z, place, :] for z in range(layers + 2 * R)]
            for z in range(layers):
                acc = None
                for k in range(KW):
                    term = taps_ref[0, 0, k] * values[z + 2 * R - k if mirror else z + k]
                    acc = term if acc is None else acc + term
                store(z, place, pl.ds(i * 8, 8), acc)
            return carry
        for i in range(piece // 8):
            tile(i, 0)

    def store_conv(z, place, local, value):
        conv[z, local, :] = value

    def along_x(value, ref):
        h, l = split(value.reshape(slab * piece, width))
        o = jnp.dot(jnp.concatenate([h, l], 1), ref[...], preferred_element_type=F32)
        return (o[:, :width] + o[:, width:]).reshape(slab, piece, width)

    def along_y(values, ref):
        parts = [split(value) for value in values]
        data = jnp.concatenate(
            [jnp.concatenate([p[0] for p in parts], 1), jnp.concatenate([p[1] for p in parts], 1)], 0)
        o = jnp.dot(ref[...], data, preferred_element_type=F32)
        o = o[:rows] + o[rows:]
        return [o[:, j * width:(j + 1) * width] for j in range(len(values))]

    def ratios(start):
        blurred = along_y([blur[start + j] for j in range(GROUP)], fy)
        ratio = [rec_ref[start + j] / blurred[j] for j in range(GROUP)]
        for j, value in enumerate(along_y(ratio, gy)):
            blur[start + j] = value

    def arrive(i, k):
        if not (isinstance(k, int) and k == 0):
            gather(i, k).wait_recv()
        guarded(i, lambda: est_halo(i, k).start())

    def arrive_across():
        arrive(first, 0)
        arrive(first, XS)
        if GATHER_BY:
            each(XS + 1, views, lambda k: relay(k).start())

    if EARLY:
        arrive_across()

    def iteration(t, carry):
        if not EARLY:
            arrive_across()

        def forward(k):
            for i in ORDER:
                guarded(i, lambda: est_halo(i, k).wait_recv())
            owner = peer(k, -1)
            convolve(whole, owner, 0, slab, False, store_conv)
            blur[:, at(owner), :] = along_x(conv[...], fx)

        if GATHER_BY:
            each(1, XS, lambda k: arrive(first, k))
            each(XS + 1, views, lambda k: arrive(first, k))
        else:
            each(2, views, lambda k: arrive(first, turn(k)))
        arrive(second, 0)

        def arrive_second(k):
            arrive(second, turn(k))

            @pl.when(k == LAG)
            def _():
                forward(0)

            @pl.when(k > LAG)
            def _():
                forward(turn(k - LAG))

        each(1, views, arrive_second)
        each(views - LAG, views, lambda k: forward(turn(k)))

        @pl.when(t == 0)
        def _():
            record.wait()

        for start in range(0, slab, GROUP):
            ratios(start)

        def last_band(k):
            owner = peer(k, 1)
            back[pl.ds(R, slab), at(owner), :] = along_x(blur[:, at(owner), :], gx)
            for i in range(2):
                guarded(i, lambda: back_halo(i, k).start())

        for k in (5, 6, 7, 1, 2, 3, 4):
            last_band(k)
        last_band(0)

        def sent(k):
            for i in range(2):
                guarded(i, lambda: est_halo(i, k).wait_send())

        each(0, views, sent)
        for i in range(2):
            each(1, views, lambda k: gather(i, k).wait_send())

        def backward(i, k, own_piece):
            def store_logs(z, place, local, value):
                logs[begin[i] + z, place, :] = flag * jnp.log(value)

            def store_own(z, place, local, value):
                sums[i, 0, z, local, :] = flag * jnp.log(value)

            guarded(i, lambda: back_halo(i, k).wait_recv())
            convolve(back, peer(k, 1), begin[i], R, True, store_own if own_piece else store_logs)

        def direct(i, k):
            backward(i, k, False)
            scatter(i, k, k).start()

        def across(k):
            backward(first, k, False)
            scatter(first, k, k % XS).start()

        def pass_on():
            each(XS + 1, views, lambda k: scatter(first, k, k).wait_recv())
            place = (pl.ds(begin[first], R), at(peer(XS, 1)))
            passed = logs[place]
            for k in range(XS + 1, views):
                passed = passed + sums[first, k]
            logs[place] = passed
            scatter(first, XS, XS).start()

        for step in PLAN:
            step_class = first if step[0] == "1" else second
            run = across if step[0] == "1" else functools.partial(direct, second)
            if step[1] == "x":
                each(1, XS, run)
            elif step[1] == "d":
                each(XS + 1, views, run)
            elif step[1] == "y" and step[0] == "1":
                backward(first, XS, False)
            elif step[1] == "y":
                run(XS)
            elif step[1] == "o":
                backward(step_class, 0, True)
            else:
                pass_on()

        for i in ORDER:
            last = XS + 1 if i == first else views
            each(1, last, lambda k: scatter(i, k, k).wait_recv())
            merged = sums[i, 0]
            for k in range(1, last):
                merged = merged + sums[i, k]
            mine = pl.ds(begin[i], R)
            own[mine] = own[mine] * jnp.exp(merged / jnp.full(merged.shape, count, F32))

            @pl.when(t < ITERS - 1)
            def _():
                send_own(i)
                if EARLY and i == first:
                    arrive_across()

        def finished(k):
            for i in range(2):
                guarded(i, lambda: back_halo(i, k).wait_send())

        each(0, views, finished)
        for i in range(2):
            each(1, views, lambda k: scatter(i, k, k).wait_send())
        return carry

    lax.fori_loop(0, ITERS, iteration, 0)
    out_ref[...] = own[...]


def shards(bricks, views, estimate, views_data, psf_taps, view_offsets, coverage):
    slab, piece, width = estimate.shape
    rows = piece * views
    dma = pltpu.SemaphoreType.DMA((2, views))
    return pl.pallas_call(
        functools.partial(kernel, bricks, views),
        out_shape=jax.ShapeDtypeStruct(estimate.shape, F32),
        in_specs=[pl.BlockSpec(memory_space=pl.ANY)] * 2
        + [pl.BlockSpec(memory_space=pltpu.SMEM)] * 3,
        out_specs=pl.BlockSpec(memory_space=pltpu.VMEM),
        scratch_shapes=[
            pltpu.VMEM((slab, rows, width), F32),
            pltpu.VMEM((slab, piece, width), F32),
            pltpu.VMEM((slab + 2 * R, rows, width), F32),
            pltpu.VMEM((slab, rows, width), F32),
            pltpu.VMEM((slab + 2 * R, rows, width), F32),
            pltpu.VMEM((slab, rows, width), F32),
            pltpu.VMEM((2, views, R, piece, width), F32),
            pltpu.VMEM((slab, piece, width), F32),
        ] + [pltpu.VMEM((2 * rows, 2 * rows), BF16)] * 4 + [dma] * 8 + [pltpu.SemaphoreType.DMA] * 2,
        compiler_params=pltpu.CompilerParams(
            collective_id=0, has_side_effects=True, vmem_limit_bytes=60 << 20),
        name="deconvolve",
    )(estimate, views_data, jnp.transpose(psf_taps, (1, 0, 2)), view_offsets, coverage)


def solution(mesh):
    return jax.shard_map(
        functools.partial(shards, mesh.shape["brick"], mesh.shape["view"]),
        mesh=mesh,
        in_specs=(
            P("brick", "view", None),
            P("view", "brick", None, None),
            P("view", None, None),
            P("view", None),
            P("brick", None),
        ),
        out_specs=P("brick", "view", None),
        check_vma=False,
    )
```
